32 devices in a mesh: role: 4 (over y, x), dp: 8 (over z, core).
Axes of the slice: x: 2, y: 2, z: 4, core: 2. Of those that a mesh axis runs over, the one named last changes fastest.
Arguments:
- wavlm_hidden: bfloat16 [16, 512, 1024], P('dp'), may hold values from -6 to 6
- whisper_hidden: bfloat16 [16, 512, 1280], P('dp'), may hold values from -6 to 6
- wavlm_qkv: bfloat16 [1024, 3072], P(None, 'dp'), may hold values from -8 to 8
- whisper_qkv: bfloat16 [1280, 3840], P(None, 'dp'), may hold values from -8 to 8
- wavlm_out: bfloat16 [1024, 1024], replicated, may hold values from -0.1875 to 0.1875
- whisper_out: bfloat16 [1280, 1280], replicated, may hold values from -0.15625 to 0.15625
- frames_valid: int32 [16], replicated, may hold values from 128 to 512, as said below
- slot_clip: int32 [16], replicated, may hold values from 0 to 15, each once
- latent: bfloat16 [2, 8, 128, 512], P(None, 'dp'), may hold values from -6 to 6
- wavlm_head: bfloat16 [512, 1024], replicated, may hold values from -0.25 to 0.25
- whisper_head: bfloat16 [512, 1280], replicated, may hold values from -0.25 to 0.25
Outputs:
- grad_wavlm_head: float32 [512, 1024], replicated
- grad_whisper_head: float32 [512, 1280], replicated
The draws below stay inside these ranges and needn't reach their ends.
Inputs may be any that keep to these rules, and one draw needn't show every extreme that they name: `frames_valid`: a multiple of 4; some clip has all 512 frames valid. `slot_clip`: every clip stands in exactly one slot.
All inputs are finite; a program needn't handle non-finite values.
Results may differ from the reference program's by a relative error of at most 0.002.
Values may be sent and summed in bfloat16 or wider, within the bound.
A program may use at most 128 MiB of HBM per device.

```python
import jax
import jax.numpy as jnp
from jax import lax

WAVLM_D = 1024
WHISPER_D = 1280
STU_D = 512
HEAD = 64
FRAMES = 512
POOL = 4
POOLED = 128
CLIPS = 16


def projection_draw(key, full_width):
    normal_key = jax.random.fold_in(jax.random.fold_in(key, 31), 0)
    weight = jax.random.normal(normal_key, (full_width, 3 * full_width), jnp.float32) * full_width ** (-0.5)
    return jnp.clip(weight, -8.0, 8.0).astype(jnp.bfloat16)


def draw_wavlm_qkv(key, part):
    return projection_draw(jax.random.fold_in(key, 5), WAVLM_D)


def draw_whisper_qkv(key, part):
    return projection_draw(jax.random.fold_in(key, 9), WHISPER_D)


def draw_frames_valid(key, part):
    count_key, full_key = jax.random.split(jax.random.fold_in(key, 17))
    pooled_counts = jax.random.randint(count_key, (CLIPS,), POOLED // 4, POOLED + 1)
    longest = jax.random.randint(full_key, (), 0, CLIPS)
    pooled_counts = pooled_counts.at[longest].set(POOLED)
    return (pooled_counts * POOL).astype(jnp.int32)


def steps_of(own_key, extent, shards, smallest, largest):
    gain = 1.0
    for dim, shards_of in shards:
        draws = jax.random.uniform(jax.random.fold_in(jax.random.fold_in(own_key, 6), dim), (shards_of,), jnp.float32, smallest / len(shards), largest / len(shards))
        gain = gain * jnp.repeat(jnp.exp(draws), extent[dim] // shards_of).reshape((-1,) + (1,) * (len(extent) - 1 - dim))
    return gain


def scatter_about(stream_key, shape, deviation, limit, shards=(), held_as=jnp.bfloat16):
    values = deviation * jax.random.normal(stream_key, shape, jnp.float32)
    if shards:
        values = values * steps_of(stream_key, shape, shards, -0.22, 0.18)
    return jnp.clip(values, -limit, limit).astype(held_as)


def setup_inputs(seed: int = 0) -> dict:
    seeds = jax.random.split(jax.random.key(seed), 12)
    wavlm_hidden = scatter_about(seeds[0], (CLIPS, FRAMES, WAVLM_D), 1.0, 6.0, ((0, 8),))
    whisper_hidden = scatter_about(seeds[1], (CLIPS, FRAMES, WHISPER_D), 1.0, 6.0, ((0, 8),))
    wavlm_qkv = draw_wavlm_qkv(jax.random.fold_in(seeds[11], 71), 0)
    whisper_qkv = draw_whisper_qkv(jax.random.fold_in(seeds[11], 71), 0)
    wavlm_out = scatter_about(seeds[4], (WAVLM_D, WAVLM_D), WAVLM_D ** -0.5, 0.1875)
    whisper_out = scatter_about(seeds[5], (WHISPER_D, WHISPER_D), WHISPER_D ** -0.5, 0.15625)
    frames_valid = draw_frames_valid(jax.random.fold_in(seeds[11], 71), 0)
    slot_clip = jax.random.permutation(seeds[7], CLIPS).astype(jnp.int32)
    latent = scatter_about(seeds[8], (2, CLIPS // 2, POOLED, STU_D), 1.0, 6.0, ((1, 8),))
    wavlm_head = scatter_about(seeds[9], (STU_D, WAVLM_D), STU_D ** -0.5, 0.25)
    whisper_head = scatter_about(seeds[10], (STU_D, WHISPER_D), STU_D ** -0.5, 0.25)
    return {"wavlm_hidden": wavlm_hidden, "whisper_hidden": whisper_hidden, "wavlm_qkv": wavlm_qkv, "whisper_qkv": whisper_qkv, "wavlm_out": wavlm_out, "whisper_out": whisper_out, "frames_valid": frames_valid, "slot_clip": slot_clip, "latent": latent, "wavlm_head": wavlm_head, "whisper_head": whisper_head}


epsilon_norm = 1e-05
epsilon_cos = 1e-06

def layer_norm(hidden):
    hidden_f = hidden.astype(jnp.float32)
    centred = hidden_f - lax.optimization_barrier(jnp.mean(hidden_f, axis=-1, keepdims=True))
    variance = lax.optimization_barrier(jnp.mean(centred * centred, axis=-1, keepdims=True))
    return (centred * lax.rsqrt(variance + epsilon_norm)).astype(jnp.bfloat16)

def teacher_clip(hidden, valid_frames, qkv_weight, out_weight):
    full_width = hidden.shape[-1]
    head_count = full_width // HEAD
    frame_count = hidden.shape[0]
    normed = layer_norm(hidden)
    projected = jnp.dot(normed, qkv_weight, preferred_element_type=jnp.float32).astype(jnp.bfloat16)
    query_rows = projected[:, :full_width].reshape(frame_count, head_count, HEAD).astype(jnp.float32)
    key_rows = projected[:, full_width:2 * full_width].reshape(frame_count, head_count, HEAD).astype(jnp.float32)
    value_rows = projected[:, 2 * full_width:].reshape(frame_count, head_count, HEAD).astype(jnp.float32)
    scores = jnp.einsum('qhd,khd->hqk', query_rows, key_rows) * HEAD ** (-0.5)
    key_mask = jnp.arange(frame_count) < valid_frames
    scores = jnp.where(key_mask[None, None, :], scores, -1e+30)
    row_max = lax.optimization_barrier(jnp.max(scores, axis=-1, keepdims=True))
    raised = jnp.exp(scores - row_max)
    weights = (raised / lax.optimization_barrier(jnp.sum(raised, axis=-1, keepdims=True))).astype(jnp.bfloat16)
    attended = jnp.einsum('hqk,khd->qhd', weights.astype(jnp.float32), value_rows)
    attended = attended.astype(jnp.bfloat16).reshape(frame_count, full_width)
    result = hidden.astype(jnp.float32) + jnp.dot(attended, out_weight, preferred_element_type=jnp.float32)
    return lax.optimization_barrier(jnp.mean(result.reshape(frame_count // POOL, POOL, full_width), axis=1)).astype(jnp.bfloat16)

def head_gradient(latent_rows, target_rows, head_weight, row_mask):
    predicted = jnp.dot(latent_rows, head_weight, preferred_element_type=jnp.float32)
    target_f = target_rows.astype(jnp.float32)
    width_scale = 1.0 / target_rows.shape[-1]
    pred_norm = jnp.sqrt(lax.optimization_barrier(jnp.sum(predicted * predicted, axis=-1)) + epsilon_cos)
    target_norm = jnp.sqrt(lax.optimization_barrier(jnp.sum(target_f * target_f, axis=-1)) + epsilon_cos)
    cosine = lax.optimization_barrier(jnp.sum(predicted * target_f, axis=-1)) / (pred_norm * target_norm)
    slope = (cosine / (pred_norm * pred_norm))[:, None] * predicted - target_f / (pred_norm * target_norm)[:, None]
    slope = slope + (predicted - target_f) * width_scale
    slope = jnp.where(row_mask[:, None], slope, 0.0).astype(jnp.bfloat16)
    return jnp.einsum('nd,nw->dw', latent_rows.astype(jnp.float32), slope.astype(jnp.float32))

def reference(wavlm_hidden, whisper_hidden, wavlm_qkv, whisper_qkv, wavlm_out, whisper_out, frames_valid, slot_clip, latent, wavlm_head, whisper_head):

    def wavlm_one(clip_args):
        return teacher_clip(clip_args[0], clip_args[1], wavlm_qkv, wavlm_out)

    def whisper_one(clip_args):
        return teacher_clip(clip_args[0], clip_args[1], whisper_qkv, whisper_out)
    wavlm_pooled = lax.map(wavlm_one, (wavlm_hidden, frames_valid))
    whisper_pooled = lax.map(whisper_one, (whisper_hidden, frames_valid))
    wavlm_target = jnp.take(wavlm_pooled, slot_clip, axis=0).reshape(CLIPS * POOLED, WAVLM_D)
    whisper_target = jnp.take(whisper_pooled, slot_clip, axis=0).reshape(CLIPS * POOLED, WHISPER_D)
    latent_rows = latent.reshape(CLIPS * POOLED, STU_D)
    slot_valid = jnp.take(frames_valid, slot_clip) // POOL
    row_mask = (jnp.arange(POOLED)[None, :] < slot_valid[:, None]).reshape(-1)
    grad_wavlm = head_gradient(latent_rows, wavlm_target, wavlm_head, row_mask)
    grad_whisper = head_gradient(latent_rows, whisper_target, whisper_head, row_mask)
    return (grad_wavlm, grad_whisper)
```

```python
import functools

import numpy as np

import jax
import jax.numpy as jnp
from jax import lax
from jax.experimental import pallas as pl
from jax.experimental.pallas import tpu as pltpu
from jax.sharding import PartitionSpec as P

HEAD = 64
POOL = 4
LOG2E = 1.4426950408889634

epsilon_norm = 1e-05
epsilon_cos = 1e-06


def column_tables(width, shards, roles):
    total = 3 * width
    per_shard = total // shards
    column = np.arange(total)
    role_of = ((column % width) // HEAD) % roles
    counts = [
        np.sum(role_of[s * per_shard : (s + 1) * per_shard] == r)
        for r in range(roles)
        for s in range(shards)
    ]
    slots = -(-int(max(counts)) // HEAD) * HEAD
    send = np.full((roles, shards, slots), -1, np.int32)
    where = np.zeros(total, np.int32)
    for r in range(roles):
        for s in range(shards):
            local = np.nonzero(role_of[s * per_shard : (s + 1) * per_shard] == r)[0]
            send[r, s, : local.size] = local
            where[s * per_shard + local] = s * slots + np.arange(local.size)
    receive = np.stack([where[role_of == r] for r in range(roles)])
    return send, receive.astype(np.int32)


def teacher_kernel(valid_ref, table_ref, hidden_ref, gathered_ref, out_ref, weight, projected, attended):
    clip = pl.program_id(0)
    width, columns = gathered_ref.shape
    needed = weight.shape[1]
    mine = needed // 3
    frames = hidden_ref.shape[1]
    rows = 128

    @pl.when(clip == 0)
    def _():
        place = lax.broadcasted_iota(jnp.int32, (columns, needed), 0) == table_ref[...]
        place = place.astype(jnp.float32).astype(jnp.bfloat16)

        @pl.loop(0, width // 256)
        def _(i):
            part = pl.ds(pl.multiple_of(i * 256, 256), 256)
            weight[part, :] = jnp.dot(
                gathered_ref[part, :], place, preferred_element_type=jnp.float32
            ).astype(jnp.bfloat16)

    @pl.loop(0, frames // rows)
    def _(i):
        part = pl.ds(pl.multiple_of(i * rows, rows), rows)
        hidden = hidden_ref[0, part, :].astype(jnp.float32)
        centred = hidden - jnp.mean(hidden, axis=-1, keepdims=True)
        variance = jnp.mean(centred * centred, axis=-1, keepdims=True)
        normed = (centred * lax.rsqrt(variance + epsilon_norm)).astype(jnp.bfloat16)
        projected[part, :] = jnp.dot(
            normed, weight[...], preferred_element_type=jnp.float32
        ).astype(jnp.bfloat16)

    key_index = lax.broadcasted_iota(jnp.int32, (1, frames), 1)
    bias = jnp.where(key_index < valid_ref[clip], 0.0, -1e30)
    ones = jnp.ones((frames, HEAD), jnp.bfloat16)
    scale = HEAD ** (-0.5) * LOG2E
    half = 256
    for j in range(mine // HEAD):
        lanes = slice(j * HEAD, (j + 1) * HEAD)
        keys = projected[:, mine + j * HEAD : mine + (j + 1) * HEAD]
        values = projected[:, 2 * mine + j * HEAD : 2 * mine + (j + 1) * HEAD]
        values = jnp.concatenate([values, ones], axis=1)
        for h in range(frames // half):
            query = projected[h * half : (h + 1) * half, lanes]
            scores = lax.dot_general(
                query, keys, (((1,), (1,)), ((), ())), preferred_element_type=jnp.float32
            )
            scores = scores + bias
            top = jnp.max(scores, axis=-1, keepdims=True)
            raised = jnp.exp2((scores - top) * scale).astype(jnp.bfloat16)
            both = jnp.dot(raised, values, preferred_element_type=jnp.float32)
            attended[h * half : (h + 1) * half, lanes] = (
                both[:, :HEAD] / both[:, HEAD : HEAD + 1]
            ).astype(jnp.bfloat16)

    pooled = frames // POOL
    row = lax.broadcasted_iota(jnp.int32, (pooled, frames), 0)
    column = lax.broadcasted_iota(jnp.int32, (pooled, frames), 1)
    average = jnp.where(column // POOL == row, 1.0 / POOL, 0.0).astype(jnp.bfloat16)
    out_ref[0] = jnp.dot(average, attended[...], preferred_element_type=jnp.float32).astype(
        jnp.bfloat16
    )


def teacher(hidden, gathered, table, valid):
    clips, frames, width = hidden.shape
    columns = gathered.shape[1]
    needed = table.shape[1]
    mine = needed // 3
    return pl.pallas_call(
        teacher_kernel,
        grid=(clips,),
        out_shape=jax.ShapeDtypeStruct((clips, frames // POOL, mine), jnp.bfloat16),
        in_specs=[
            pl.BlockSpec(memory_space=pltpu.SMEM),
            pl.BlockSpec((1, needed), lambda i: (0, 0)),
            pl.BlockSpec((1, frames, width), lambda i: (i, 0, 0)),
            pl.BlockSpec((width, columns), lambda i: (0, 0)),
        ],
        out_specs=pl.BlockSpec((1, frames // POOL, mine), lambda i: (i, 0, 0)),
        scratch_shapes=[
            pltpu.VMEM((width, needed), jnp.bfloat16),
            pltpu.VMEM((frames, needed), jnp.bfloat16),
            pltpu.VMEM((frames, mine), jnp.bfloat16),
        ],
        compiler_params=pltpu.CompilerParams(vmem_limit_bytes=40 * 1024 * 1024),
        cost_estimate=pl.CostEstimate(
            flops=2 * clips * frames * needed * (width + frames),
            bytes_accessed=2 * width * (columns + clips * frames),
            transcendentals=clips * frames * frames * mine // HEAD,
        ),
    )(valid, table, hidden, gathered)


def slope_of(latent_rows, target, head_weight, row_mask):
    predicted = jnp.dot(latent_rows, head_weight, preferred_element_type=jnp.float32)
    target_f = target.astype(jnp.float32)
    width_scale = 1.0 / target.shape[-1]
    pred_norm = jnp.sqrt(jnp.sum(predicted * predicted, axis=-1) + epsilon_cos)
    target_norm = jnp.sqrt(jnp.sum(target_f * target_f, axis=-1) + epsilon_cos)
    cosine = jnp.sum(predicted * target_f, axis=-1) / (pred_norm * target_norm)
    slope = (cosine / (pred_norm * pred_norm))[:, None] * predicted - target_f / (
        pred_norm * target_norm
    )[:, None]
    slope = slope + (predicted - target_f) * width_scale
    return jnp.where(row_mask[:, None], slope, 0.0).astype(jnp.bfloat16)


def per_device(
    wavlm_hidden,
    whisper_hidden,
    wavlm_qkv,
    whisper_qkv,
    wavlm_out,
    whisper_out,
    frames_valid,
    slot_clip,
    latent,
    wavlm_head,
    whisper_head,
):
    role = lax.axis_index("role")
    column = lax.axis_index("dp")
    roles = lax.axis_size("role")
    dp_count = lax.axis_size("dp")
    devices = roles * dp_count
    clips_here, frames = wavlm_hidden.shape[:2]
    pooled = frames // POOL
    quarter = pooled // roles
    stu = latent.shape[-1]
    all_clips = frames_valid.shape[0]
    valid_here = lax.dynamic_slice_in_dim(frames_valid, column * clips_here, clips_here)

    def my_columns(shard, width):
        send, receive = column_tables(width, dp_count, roles)
        wanted = jnp.asarray(send)[role, column]
        place = jnp.arange(shard.shape[1])[:, None] == wanted[None, :]
        picked = jnp.dot(shard, place.astype(jnp.bfloat16), preferred_element_type=jnp.float32)
        return picked.astype(jnp.bfloat16), jnp.asarray(receive)[role][None, :]

    wavlm_width = wavlm_hidden.shape[-1]
    whisper_width = whisper_hidden.shape[-1]
    wavlm_part, wavlm_table = my_columns(wavlm_qkv, wavlm_width)
    whisper_part, whisper_table = my_columns(whisper_qkv, whisper_width)
    wavlm_all, whisper_all, latent_all = lax.all_gather(
        (wavlm_part, whisper_part, latent), "dp", axis=1, tiled=True
    )

    wavlm_att = teacher(wavlm_hidden, wavlm_all, wavlm_table, valid_here)
    whisper_att = teacher(whisper_hidden, whisper_all, whisper_table, valid_here)
    att = jnp.concatenate([wavlm_att, whisper_att], axis=-1)
    mine = att.shape[-1]
    att = att.reshape(clips_here, roles, quarter, mine).transpose(1, 0, 2, 3)
    att = lax.all_to_all(att, "role", split_axis=0, concat_axis=0, tiled=True)
    att = att.reshape(roles, clips_here * quarter, mine)

    slots = jnp.arange(all_clips)
    slot_of = jnp.sum(jnp.where(slot_clip[None, :] == slots[:, None], slots[None, :], 0), axis=1)
    latent_by_clip = jnp.take(latent_all.reshape(all_clips, pooled, stu), slot_of, axis=0)
    latent_rows = lax.dynamic_slice(
        latent_by_clip, (column * clips_here, role * quarter, 0), (clips_here, quarter, stu)
    ).reshape(clips_here * quarter, stu)
    row_mask = (
        (role * quarter + jnp.arange(quarter))[None, :] < (valid_here // POOL)[:, None]
    ).reshape(-1)

    def slope_teacher(hidden, att_rows, out_weight, head_weight):
        width = hidden.shape[-1]
        here = lax.dynamic_slice_in_dim(hidden, role * quarter * POOL, quarter * POOL, 1)
        here = jnp.mean(
            here.astype(jnp.float32).reshape(clips_here * quarter, POOL, width), axis=1
        )
        weight = out_weight.reshape(-1, roles, HEAD, width).transpose(1, 0, 2, 3)
        weight = weight.reshape(width, width)
        rows = att_rows.transpose(1, 0, 2).reshape(clips_here * quarter, width)
        target = here + jnp.dot(rows, weight, preferred_element_type=jnp.float32)
        return slope_of(latent_rows, target.astype(jnp.bfloat16), head_weight, row_mask)

    split = wavlm_att.shape[-1]
    slope = jnp.concatenate(
        [
            slope_teacher(wavlm_hidden, att[:, :, :split], wavlm_out, wavlm_head),
            slope_teacher(whisper_hidden, att[:, :, split:], whisper_out, whisper_head),
        ],
        axis=1,
    )
    block = slope.shape[1] // devices
    slope = slope.reshape(-1, devices, block).transpose(1, 0, 2)
    slope = lax.all_to_all(slope, ("role", "dp"), split_axis=0, concat_axis=0, tiled=True)
    slope = slope.reshape(roles, dp_count, clips_here, quarter, block).transpose(1, 2, 0, 3, 4)
    slope = slope.reshape(all_clips * pooled, block)
    grad = lax.dot_general(
        slope,
        latent_by_clip.reshape(all_clips * pooled, stu),
        (((0,), (0,)), ((), ())),
        preferred_element_type=jnp.float32,
    )
    grad = lax.all_gather(grad, ("role", "dp"), axis=0, tiled=True)
    return grad[:wavlm_width].T, grad[wavlm_width:].T


def solution(mesh):
    in_specs = (
        P("dp", None, None),
        P("dp", None, None),
        P(None, "dp"),
        P(None, "dp"),
        P(),
        P(),
        P(),
        P(),
        P(None, "dp", None, None),
        P(),
        P(),
    )
    out_specs = (P(), P())
    return jax.shard_map(
        per_device, mesh=mesh, in_specs=in_specs, out_specs=out_specs, check_vma=False
    )
```

```python
import functools

import numpy as np

import jax
import jax.numpy as jnp
from jax import lax
from jax.experimental import pallas as pl
from jax.experimental.pallas import tpu as pltpu
from jax.sharding import PartitionSpec as P

HEAD = 64
POOL = 4
LANES = 128
LOG2E = 1.4426950408889634

epsilon_norm = 1e-05
epsilon_cos = 1e-06


def column_tables(width, shards, roles):
    total = 3 * width
    per_shard = total // shards
    column = np.arange(total)
    role_of = ((column % width) // HEAD) % roles
    counts = [
        np.sum(role_of[s * per_shard : (s + 1) * per_shard] == r)
        for r in range(roles)
        for s in range(shards)
    ]
    slots = -(-int(max(counts)) // LANES) * LANES
    send = np.full((roles, shards, slots), -1, np.int32)
    where = np.zeros(total, np.int32)
    for r in range(roles):
        for s in range(shards):
            local = np.nonzero(role_of[s * per_shard : (s + 1) * per_shard] == r)[0]
            send[r, s, : local.size] = local
            where[s * per_shard + local] = s * slots + np.arange(local.size)
    receive = np.stack([where[role_of == r] for r in range(roles)])
    return send, receive.astype(np.int32)


def teacher_kernel(
    first, valid_ref, table_ref, hidden_ref, gathered_ref, out_ref,
    held, place, weight, projected, attended, copied,
):
    clip = pl.program_id(0)
    shards, width, slots = held.shape
    columns = shards * slots
    needed = weight.shape[1]
    mine = needed // 3
    frames = hidden_ref.shape[1]
    rows = 128

    @pl.when(clip == 0)
    def _():
        copy = pltpu.make_async_copy(gathered_ref.at[:, pl.ds(first, width), :], held, copied)
        copy.start()

        @pl.loop(0, columns // LANES)
        def _(i):
            start = pl.multiple_of(i * LANES, LANES)
            row = lax.broadcasted_iota(jnp.int32, (LANES, needed), 0) + start
            place[pl.ds(start, LANES), :] = (
                (row == table_ref[...]).astype(jnp.float32).astype(jnp.bfloat16)
            )

        copy.wait()

        @pl.loop(0, width // 256)
        def _(i):
            part = pl.ds(pl.multiple_of(i * 256, 256), 256)
            joined = jnp.concatenate([held[s, part, :] for s in range(shards)], axis=1)
            weight[part, :] = jnp.dot(
                joined, place[...], preferred_element_type=jnp.float32
            ).astype(jnp.bfloat16)

    @pl.loop(0, frames // rows)
    def _(i):
        part = pl.ds(pl.multiple_of(i * rows, rows), rows)
        hidden = hidden_ref[0, part, :].astype(jnp.float32)
        centred = hidden - jnp.mean(hidden, axis=-1, keepdims=True)
        variance = jnp.mean(centred * centred, axis=-1, keepdims=True)
        normed = (centred * lax.rsqrt(variance + epsilon_norm)).astype(jnp.bfloat16)
        projected[part, :] = jnp.dot(
            normed, weight[...], preferred_element_type=jnp.float32
        ).astype(jnp.bfloat16)

    key_index = lax.broadcasted_iota(jnp.int32, (1, frames), 1)
    bias = jnp.where(key_index < valid_ref[clip], 0.0, -1e30)
    scale = HEAD ** (-0.5) * LOG2E
    half = 256
    for j in range(mine // HEAD):
        lanes = slice(j * HEAD, (j + 1) * HEAD)
        keys = projected[:, mine + j * HEAD : mine + (j + 1) * HEAD]
        values = projected[:, 2 * mine + j * HEAD : 2 * mine + (j + 1) * HEAD]
        for h in range(frames // half):
            query = projected[h * half : (h + 1) * half, lanes]
            scores = lax.dot_general(
                query, keys, (((1,), (1,)), ((), ())), preferred_element_type=jnp.float32
            )
            scores = scores + bias
            top = jnp.max(scores, axis=-1, keepdims=True)
            raised = jnp.exp2((scores - top) * scale)
            weights = raised * (1.0 / jnp.sum(raised, axis=-1, keepdims=True))
            attended[h * half : (h + 1) * half, lanes] = jnp.dot(
                weights.astype(jnp.bfloat16), values, preferred_element_type=jnp.float32
            ).astype(jnp.bfloat16)

    pooled = frames // POOL
    row = lax.broadcasted_iota(jnp.int32, (pooled, frames), 0)
    column = lax.broadcasted_iota(jnp.int32, (pooled, frames), 1)
    average = jnp.where(column // POOL == row, 1.0 / POOL, 0.0).astype(jnp.bfloat16)
    mean = jnp.dot(average, attended[...], preferred_element_type=jnp.float32)
    high = mean.astype(jnp.bfloat16)
    out_ref[0, :, :mine] = high
    out_ref[0, :, mine:] = (mean - high.astype(jnp.float32)).astype(jnp.bfloat16)


def teacher(hidden, gathered, first, table, valid):
    clips, frames, width = hidden.shape
    shards, _, slots = gathered.shape
    columns = shards * slots
    needed = table.shape[1]
    mine = needed // 3
    return pl.pallas_call(
        functools.partial(teacher_kernel, first),
        grid=(clips,),
        out_shape=jax.ShapeDtypeStruct((clips, frames // POOL, 2 * mine), jnp.bfloat16),
        in_specs=[
            pl.BlockSpec(memory_space=pltpu.SMEM),
            pl.BlockSpec((1, needed), lambda i: (0, 0)),
            pl.BlockSpec((1, frames, width), lambda i: (i, 0, 0)),
            pl.BlockSpec(memory_space=pl.ANY),
        ],
        out_specs=pl.BlockSpec((1, frames // POOL, 2 * mine), lambda i: (i, 0, 0)),
        scratch_shapes=[
            pltpu.VMEM((shards, width, slots), jnp.bfloat16),
            pltpu.VMEM((columns, needed), jnp.bfloat16),
            pltpu.VMEM((width, needed), jnp.bfloat16),
            pltpu.VMEM((frames, needed), jnp.bfloat16),
            pltpu.VMEM((frames, mine), jnp.bfloat16),
            pltpu.SemaphoreType.DMA,
        ],
        compiler_params=pltpu.CompilerParams(vmem_limit_bytes=48 * 1024 * 1024),
        cost_estimate=pl.CostEstimate(
            flops=2 * clips * frames * needed * (width + frames),
            bytes_accessed=2 * width * (columns + clips * frames),
            transcendentals=clips * frames * frames * mine // HEAD,
        ),
    )(valid, table, hidden, gathered)


def slope_of(latent_rows, target, head_weight, row_mask):
    predicted = jnp.dot(latent_rows, head_weight, preferred_element_type=jnp.float32)
    target_f = target.astype(jnp.float32)
    width_scale = 1.0 / target.shape[-1]
    pred_norm = jnp.sqrt(jnp.sum(predicted * predicted, axis=-1) + epsilon_cos)
    target_norm = jnp.sqrt(jnp.sum(target_f * target_f, axis=-1) + epsilon_cos)
    cosine = jnp.sum(predicted * target_f, axis=-1) / (pred_norm * target_norm)
    slope = (cosine / (pred_norm * pred_norm))[:, None] * predicted - target_f / (
        pred_norm * target_norm
    )[:, None]
    slope = slope + (predicted - target_f) * width_scale
    return jnp.where(row_mask[:, None], slope, 0.0).astype(jnp.bfloat16)


def per_device(
    wavlm_hidden,
    whisper_hidden,
    wavlm_qkv,
    whisper_qkv,
    wavlm_out,
    whisper_out,
    frames_valid,
    slot_clip,
    latent,
    wavlm_head,
    whisper_head,
):
    role = lax.axis_index("role")
    column = lax.axis_index("dp")
    roles = lax.axis_size("role")
    dp_count = lax.axis_size("dp")
    devices = roles * dp_count
    clips_here, frames = wavlm_hidden.shape[:2]
    pooled = frames // POOL
    quarter = pooled // roles
    stu = latent.shape[-1]
    all_clips = frames_valid.shape[0]
    valid_here = lax.dynamic_slice_in_dim(frames_valid, column * clips_here, clips_here)

    def my_columns(shard, width):
        send, receive = column_tables(width, dp_count, roles)
        wanted = jnp.asarray(send)[role, column]
        place = jnp.arange(shard.shape[1])[:, None] == wanted[None, :]
        picked = jnp.dot(shard, place.astype(jnp.bfloat16), preferred_element_type=jnp.float32)
        return picked.astype(jnp.bfloat16), jnp.asarray(receive)[role][None, :]

    wavlm_width = wavlm_hidden.shape[-1]
    whisper_width = whisper_hidden.shape[-1]
    wavlm_part, wavlm_table = my_columns(wavlm_qkv, wavlm_width)
    whisper_part, whisper_table = my_columns(whisper_qkv, whisper_width)
    slots = wavlm_part.shape[1]
    parts = jnp.concatenate([wavlm_part, whisper_part, latent.reshape(-1, slots)], axis=0)
    gathered = lax.all_gather(parts, "dp", axis=0, tiled=False)
    latent_all = gathered[:, wavlm_width + whisper_width :, :].reshape(
        dp_count, latent.shape[0], latent.shape[1], pooled, stu
    ).transpose(1, 0, 2, 3, 4)

    wavlm_att = teacher(wavlm_hidden, gathered, 0, wavlm_table, valid_here)
    whisper_att = teacher(whisper_hidden, gathered, wavlm_width, whisper_table, valid_here)
    att = jnp.concatenate([wavlm_att, whisper_att], axis=-1)
    mine = att.shape[-1]
    att = att.reshape(clips_here, roles, quarter, mine).transpose(1, 0, 2, 3)
    att = lax.all_to_all(att, "role", split_axis=0, concat_axis=0, tiled=True)
    att = att.reshape(roles, clips_here * quarter, mine)

    order = jnp.arange(all_clips)
    slot_of = jnp.sum(jnp.where(slot_clip[None, :] == order[:, None], order[None, :], 0), axis=1)
    latent_by_clip = jnp.take(latent_all.reshape(all_clips, pooled, stu), slot_of, axis=0)
    latent_rows = lax.dynamic_slice(
        latent_by_clip, (column * clips_here, role * quarter, 0), (clips_here, quarter, stu)
    ).reshape(clips_here * quarter, stu)
    row_mask = (
        (role * quarter + jnp.arange(quarter))[None, :] < (valid_here // POOL)[:, None]
    ).reshape(-1)

    def slope_teacher(hidden, att_rows, out_weight, head_weight):
        width = hidden.shape[-1]
        here = lax.dynamic_slice_in_dim(hidden, role * quarter * POOL, quarter * POOL, 1)
        here = jnp.mean(
            here.astype(jnp.float32).reshape(clips_here * quarter, POOL, width), axis=1
        )
        weight = out_weight.reshape(-1, roles, HEAD, width).transpose(1, 0, 2, 3)
        weight = weight.reshape(width, width)
        share = width // roles
        high, low = (
            part.transpose(1, 0, 2).reshape(clips_here * quarter, width)
            for part in (att_rows[:, :, :share], att_rows[:, :, share:])
        )
        target = jnp.dot(high, weight, preferred_element_type=jnp.float32)
        target = here + (target + jnp.dot(low, weight, preferred_element_type=jnp.float32))
        return slope_of(latent_rows, target.astype(jnp.bfloat16), head_weight, row_mask)

    split = wavlm_att.shape[-1]
    slope = jnp.concatenate(
        [
            slope_teacher(wavlm_hidden, att[:, :, :split], wavlm_out, wavlm_head),
            slope_teacher(whisper_hidden, att[:, :, split:], whisper_out, whisper_head),
        ],
        axis=1,
    )
    block = slope.shape[1] // devices
    slope = slope.reshape(-1, devices, block).transpose(1, 0, 2)
    slope = lax.all_to_all(slope, ("role", "dp"), split_axis=0, concat_axis=0, tiled=True)
    slope = slope.reshape(roles, dp_count, clips_here, quarter, block).transpose(1, 2, 0, 3, 4)
    slope = slope.reshape(all_clips * pooled, block)
    grad = lax.dot_general(
        slope,
        latent_by_clip.reshape(all_clips * pooled, stu),
        (((0,), (0,)), ((), ())),
        preferred_element_type=jnp.float32,
    )
    grad = lax.all_gather(grad, ("role", "dp"), axis=0, tiled=True)
    return grad[:wavlm_width].T, grad[wavlm_width:].T


def solution(mesh):
    in_specs = (
        P("dp", None, None),
        P("dp", None, None),
        P(None, "dp"),
        P(None, "dp"),
        P(),
        P(),
        P(),
        P(),
        P(None, "dp", None, None),
        P(),
        P(),
    )
    out_specs = (P(), P())
    return jax.shard_map(
        per_device, mesh=mesh, in_specs=in_specs, out_specs=out_specs, check_vma=False
    )
```

```python
import functools

import numpy as np

import jax
import jax.numpy as jnp
from jax import lax
from jax.experimental import pallas as pl
from jax.experimental.pallas import tpu as pltpu
from jax.sharding import PartitionSpec as P

HEAD = 64
POOL = 4
LANES = 128
LOG2E = 1.4426950408889634

epsilon_norm = 1e-05
epsilon_cos = 1e-06


def column_tables(width, shards, roles):
    total = 3 * width
    per_shard = total // shards
    column = np.arange(total)
    role_of = ((column % width) // HEAD) % roles
    counts = [
        np.sum(role_of[s * per_shard : (s + 1) * per_shard] == r)
        for r in range(roles)
        for s in range(shards)
    ]
    slots = -(-int(max(counts)) // LANES) * LANES
    send = np.full((roles, shards, slots), -1, np.int32)
    where = np.zeros(total, np.int32)
    for r in range(roles):
        for s in range(shards):
            local = np.nonzero(role_of[s * per_shard : (s + 1) * per_shard] == r)[0]
            send[r, s, : local.size] = local
            where[s * per_shard + local] = s * slots + np.arange(local.size)
    receive = np.stack([where[role_of == r] for r in range(roles)])
    return send, receive.astype(np.int32)


def teacher_kernel(
    first, valid_ref, table_ref, hidden_ref, gathered_ref, out_ref,
    held, place, weight, projected, attended, copied,
):
    clip = pl.program_id(0)
    shards, width, slots = held.shape
    columns = shards * slots
    needed = weight.shape[1]
    mine = needed // 3
    frames = hidden_ref.shape[1]
    rows = 128

    @pl.when(clip == 0)
    def _():
        copy = pltpu.make_async_copy(gathered_ref.at[:, pl.ds(first, width), :], held, copied)
        copy.start()

        @pl.loop(0, columns // LANES)
        def _(i):
            start = pl.multiple_of(i * LANES, LANES)
            row = lax.broadcasted_iota(jnp.int32, (LANES, needed), 0) + start
            place[pl.ds(start, LANES), :] = (
                (row == table_ref[...]).astype(jnp.float32).astype(jnp.bfloat16)
            )

        copy.wait()

        @pl.loop(0, width // 256)
        def _(i):
            part = pl.ds(pl.multiple_of(i * 256, 256), 256)
            joined = jnp.concatenate([held[s, part, :] for s in range(shards)], axis=1)
            weight[part, :] = jnp.dot(
                joined, place[...], preferred_element_type=jnp.float32
            ).astype(jnp.bfloat16)

    @pl.loop(0, frames // rows)
    def _(i):
        part = pl.ds(pl.multiple_of(i * rows, rows), rows)
        hidden = hidden_ref[0, part, :].astype(jnp.float32)
        centred = hidden - jnp.mean(hidden, axis=-1, keepdims=True)
        variance = jnp.mean(centred * centred, axis=-1, keepdims=True)
        normed = (centred * lax.rsqrt(variance + epsilon_norm)).astype(jnp.bfloat16)
        projected[part, :] = jnp.dot(
            normed, weight[...], preferred_element_type=jnp.float32
        ).astype(jnp.bfloat16)

    key_index = lax.broadcasted_iota(jnp.int32, (1, frames), 1)
    bias = jnp.where(key_index < valid_ref[clip], 0.0, -1e30)
    scale = HEAD ** (-0.5) * LOG2E
    half = 256
    for j in range(mine // HEAD):
        lanes = slice(j * HEAD, (j + 1) * HEAD)
        keys = projected[:, mine + j * HEAD : mine + (j + 1) * HEAD]
        values = projected[:, 2 * mine + j * HEAD : 2 * mine + (j + 1) * HEAD]
        for h in range(frames // half):
            query = projected[h * half : (h + 1) * half, lanes]
            scores = lax.dot_general(
                query, keys, (((1,), (1,)), ((), ())), preferred_element_type=jnp.float32
            )
            scores = scores + bias
            top = jnp.max(scores, axis=-1, keepdims=True)
            raised = jnp.exp2((scores - top) * scale)
            weights = raised * (1.0 / jnp.sum(raised, axis=-1, keepdims=True))
            attended[h * half : (h + 1) * half, lanes] = jnp.dot(
                weights.astype(jnp.bfloat16), values, preferred_element_type=jnp.float32
            ).astype(jnp.bfloat16)

    pooled = frames // POOL
    row = lax.broadcasted_iota(jnp.int32, (pooled, frames), 0)
    column = lax.broadcasted_iota(jnp.int32, (pooled, frames), 1)
    average = jnp.where(column // POOL == row, 1.0 / POOL, 0.0).astype(jnp.bfloat16)
    mean = jnp.dot(average, attended[...], preferred_element_type=jnp.float32)
    high = mean.astype(jnp.bfloat16)
    out_ref[0, :, :mine] = high
    out_ref[0, :, mine:] = (mean - high.astype(jnp.float32)).astype(jnp.bfloat16)


def teacher(hidden, gathered, first, table, valid):
    clips, frames, width = hidden.shape
    shards, _, slots = gathered.shape
    columns = shards * slots
    needed = table.shape[1]
    mine = needed // 3
    return pl.pallas_call(
        functools.partial(teacher_kernel, first),
        grid=(clips,),
        out_shape=jax.ShapeDtypeStruct((clips, frames // POOL, 2 * mine), jnp.bfloat16),
        in_specs=[
            pl.BlockSpec(memory_space=pltpu.SMEM),
            pl.BlockSpec((1, needed), lambda i: (0, 0)),
            pl.BlockSpec((1, frames, width), lambda i: (i, 0, 0)),
            pl.BlockSpec(memory_space=pl.ANY),
        ],
        out_specs=pl.BlockSpec((1, frames // POOL, 2 * mine), lambda i: (i, 0, 0)),
        scratch_shapes=[
            pltpu.VMEM((shards, width, slots), jnp.bfloat16),
            pltpu.VMEM((columns, needed), jnp.bfloat16),
            pltpu.VMEM((width, needed), jnp.bfloat16),
            pltpu.VMEM((frames, needed), jnp.bfloat16),
            pltpu.VMEM((frames, mine), jnp.bfloat16),
            pltpu.SemaphoreType.DMA,
        ],
        compiler_params=pltpu.CompilerParams(vmem_limit_bytes=48 * 1024 * 1024),
        cost_estimate=pl.CostEstimate(
            flops=2 * clips * frames * needed * (width + frames),
            bytes_accessed=2 * width * (columns + clips * frames),
            transcendentals=clips * frames * frames * mine // HEAD,
        ),
    )(valid, table, hidden, gathered)


def pick_kernel(*refs):
    out_ref = refs[-1]
    first = 0
    for shard_ref, table_ref in zip(refs[:-1:2], refs[1:-1:2]):
        depth, columns = shard_ref.shape
        row = lax.broadcasted_iota(jnp.int32, (columns, out_ref.shape[1]), 0)
        place = (row == table_ref[...]).astype(jnp.float32).astype(jnp.bfloat16)
        out_ref[first : first + depth, :] = jnp.dot(
            shard_ref[...], place, preferred_element_type=jnp.float32
        ).astype(jnp.bfloat16)
        first += depth


def pick(pairs):
    depth = sum(shard.shape[0] for shard, _ in pairs)
    slots = pairs[0][1].shape[1]
    operands = [array for pair in pairs for array in pair]
    return pl.pallas_call(
        pick_kernel,
        out_shape=jax.ShapeDtypeStruct((depth, slots), jnp.bfloat16),
        in_specs=[pl.BlockSpec(memory_space=pltpu.VMEM)] * len(operands),
        out_specs=pl.BlockSpec(memory_space=pltpu.VMEM),
        compiler_params=pltpu.CompilerParams(vmem_limit_bytes=24 * 1024 * 1024),
    )(*operands)


def finish_kernel(blocks_ref, *out_refs):
    first = 0
    for out_ref in out_refs:
        width = out_ref.shape[1]
        for start in range(0, width, LANES):
            part = blocks_ref[first + start : first + start + LANES, :].astype(jnp.float32)
            out_ref[:, start : start + LANES] = part.T
        first += width


def finish(blocks, widths):
    depth = blocks.shape[1]
    return pl.pallas_call(
        finish_kernel,
        out_shape=[jax.ShapeDtypeStruct((depth, width), jnp.float32) for width in widths],
        in_specs=[pl.BlockSpec(memory_space=pltpu.VMEM)],
        out_specs=[pl.BlockSpec(memory_space=pltpu.VMEM)] * len(widths),
        compiler_params=pltpu.CompilerParams(vmem_limit_bytes=32 * 1024 * 1024),
    )(blocks)


def slope_of(latent_rows, target, head_weight, row_mask):
    predicted = jnp.dot(latent_rows, head_weight, preferred_element_type=jnp.float32)
    target_f = lax.reduce_precision(target, 8, 7)
    width_scale = 1.0 / target.shape[-1]
    pred_norm = jnp.sqrt(jnp.sum(predicted * predicted, axis=-1) + epsilon_cos)
    target_norm = jnp.sqrt(jnp.sum(target_f * target_f, axis=-1) + epsilon_cos)
    cosine = jnp.sum(predicted * target_f, axis=-1) / (pred_norm * target_norm)
    slope = (cosine / (pred_norm * pred_norm))[:, None] * predicted - target_f / (
        pred_norm * target_norm
    )[:, None]
    slope = slope + (predicted - target_f) * width_scale
    return jnp.where(row_mask[:, None], slope, 0.0).astype(jnp.bfloat16)


def per_device(
    wavlm_hidden,
    whisper_hidden,
    wavlm_qkv,
    whisper_qkv,
    wavlm_out,
    whisper_out,
    frames_valid,
    slot_clip,
    latent,
    wavlm_head,
    whisper_head,
):
    role = lax.axis_index("role")
    column = lax.axis_index("dp")
    roles = lax.axis_size("role")
    dp_count = lax.axis_size("dp")
    devices = roles * dp_count
    clips_here, frames = wavlm_hidden.shape[:2]
    pooled = frames // POOL
    quarter = pooled // roles
    stu = latent.shape[-1]
    all_clips = frames_valid.shape[0]
    valid_here = lax.dynamic_slice_in_dim(frames_valid, column * clips_here, clips_here)

    def my_columns(shard, width):
        send, receive = column_tables(width, dp_count, roles)
        wanted = jnp.asarray(send)[role, column]
        return wanted[None, :], jnp.asarray(receive)[role][None, :]

    wavlm_width = wavlm_hidden.shape[-1]
    whisper_width = whisper_hidden.shape[-1]
    wavlm_wanted, wavlm_table = my_columns(wavlm_qkv, wavlm_width)
    whisper_wanted, whisper_table = my_columns(whisper_qkv, whisper_width)
    parts = pick([(wavlm_qkv, wavlm_wanted), (whisper_qkv, whisper_wanted)])
    gathered = lax.all_gather(parts, "dp", axis=0, tiled=True)
    gathered, latent = lax.optimization_barrier((gathered, latent))
    latent_all = lax.all_gather(latent.reshape(-1, stu), "dp", axis=0, tiled=True)
    gathered = gathered.reshape(dp_count, wavlm_width + whisper_width, -1)

    wavlm_att = teacher(wavlm_hidden, gathered, 0, wavlm_table, valid_here)
    whisper_att = teacher(whisper_hidden, gathered, wavlm_width, whisper_table, valid_here)
    wavlm_att, whisper_att, latent_all = lax.optimization_barrier(
        (wavlm_att, whisper_att, latent_all)
    )
    att = jnp.concatenate([wavlm_att, whisper_att], axis=-1)
    mine = att.shape[-1]
    att = att.reshape(clips_here, roles, quarter, mine).transpose(1, 0, 2, 3)
    att = lax.all_to_all(att, "role", split_axis=0, concat_axis=0, tiled=True)
    att = att.reshape(roles, clips_here * quarter, mine)

    order = jnp.arange(all_clips)
    slot_of = jnp.sum(jnp.where(slot_clip[None, :] == order[:, None], order[None, :], 0), axis=1)
    halves, owned = latent.shape[:2]
    half, rest = slot_of // (dp_count * owned), slot_of % (dp_count * owned)
    place = (rest // owned * halves + half) * owned + rest % owned
    latent_by_clip = jnp.take(latent_all.reshape(all_clips, pooled, stu), place, axis=0)
    latent_rows = lax.dynamic_slice(
        latent_by_clip, (column * clips_here, role * quarter, 0), (clips_here, quarter, stu)
    ).reshape(clips_here * quarter, stu)
    row_mask = (
        (role * quarter + jnp.arange(quarter))[None, :] < (valid_here // POOL)[:, None]
    ).reshape(-1)

    def slope_teacher(hidden, att_rows, out_weight, head_weight):
        width = hidden.shape[-1]
        here = lax.dynamic_slice_in_dim(hidden, role * quarter * POOL, quarter * POOL, 1)
        here = jnp.mean(
            here.astype(jnp.float32).reshape(clips_here * quarter, POOL, width), axis=1
        )
        weight = out_weight.reshape(-1, roles, HEAD, width).transpose(1, 0, 2, 3)
        weight = weight.reshape(width, width)
        share = width // roles
        high, low = (
            part.transpose(1, 0, 2).reshape(clips_here * quarter, width)
            for part in (att_rows[:, :, :share], att_rows[:, :, share:])
        )
        target = jnp.dot(high, weight, preferred_element_type=jnp.float32)
        target = here + (target + jnp.dot(low, weight, preferred_element_type=jnp.float32))
        return slope_of(latent_rows, target, head_weight, row_mask)

    split = wavlm_att.shape[-1]
    slope = jnp.concatenate(
        [
            slope_teacher(wavlm_hidden, att[:, :, :split], wavlm_out, wavlm_head),
            slope_teacher(whisper_hidden, att[:, :, split:], whisper_out, whisper_head),
        ],
        axis=1,
    )
    block = slope.shape[1] // devices
    slope = slope.reshape(-1, devices, block).transpose(1, 0, 2)
    slope = lax.all_to_all(slope, ("role", "dp"), split_axis=0, concat_axis=0, tiled=True)
    slope = slope.reshape(roles, dp_count, clips_here, quarter, block).transpose(1, 2, 0, 3, 4)
    slope = slope.reshape(all_clips * pooled, block)
    grad = lax.dot_general(
        slope,
        latent_by_clip.reshape(all_clips * pooled, stu),
        (((0,), (0,)), ((), ())),
        preferred_element_type=jnp.float32,
    )
    grad = lax.all_gather(grad.astype(jnp.bfloat16), ("role", "dp"), axis=0, tiled=True)
    return tuple(finish(grad, (wavlm_width, whisper_width)))


def solution(mesh):
    in_specs = (
        P("dp", None, None),
        P("dp", None, None),
        P(None, "dp"),
        P(None, "dp"),
        P(),
        P(),
        P(),
        P(),
        P(None, "dp", None, None),
        P(),
        P(),
    )
    out_specs = (P(), P())
    return jax.shard_map(
        per_device, mesh=mesh, in_specs=in_specs, out_specs=out_specs, check_vma=False
    )
```
